512 devices in a mesh: lat: 64 (over y, z), tok: 8 (over x, core).
Axes of the slice: x: 4, y: 8, z: 8, core: 2. Of those that a mesh axis runs over, the one named last changes fastest.
Arguments:
- tokens: bfloat16 [512, 9216], P(None, 'tok'), may hold values from -6 to 6
- enc_weight: bfloat16 [9216, 32768], P('tok', 'lat'), may hold values from -0.0625 to 0.0625
- enc_bias: float32 [32768], P('lat'), may hold values from -1.5 to 0.5
- dec_weight: bfloat16 [32768, 9216], P('lat', 'tok'), may hold values from -0.03125 to 0.03125
- pairs: int32 [64, 32], P('lat'), may hold values from 0 to 31, as said below
- counts: int32 [64], P('lat'), may hold values from 1 to 32, as said below
Outputs:
- error: bfloat16 [512, 9216], P('lat', 'tok')
- enc_grad: bfloat16 [9216, 32768], P('tok', 'lat')
- dec_grad: bfloat16 [32768, 9216], P('lat', 'tok')
- bias_grad: float32 [32768], P('lat')
The draws below stay inside these ranges and needn't reach their ends.
Inputs may be any that keep to these rules, and one draw needn't show every extreme that they name: `pairs`: each code is g * 8 + k for a row block g and a latent block k of the shard; the first counts[j] codes of row j are distinct; codes past counts[j] are to be ignored. `counts`: some shard has all 32 slots active.
All inputs are finite; a program needn't handle non-finite values.
Results may differ from the reference program's by a relative error of at most 0.023.
Values may be sent and summed in bfloat16 or wider, within the bound.
No kernel may reach another device: no remote copies, remote signals or barrier semaphores. Data moves between devices by JAX's collectives and lax.ppermute only.
A program may use at most 128 MiB of HBM per device.

```python
import jax
import jax.numpy as jnp
from jax import lax

D = 4608
DIN = 9216
ROWS = 512
LB = 8
BR = 128
BL = 64
RBLK = 4
PAIRS = 32
LATENTS = 32768
N_LAT = 64


def draw_pairs(key, part):
    key = jax.random.fold_in(key, 11)
    keys = jax.random.split(key, N_LAT)
    return jax.vmap(lambda one: jax.random.permutation(one, PAIRS))(keys).astype(jnp.int32)


def draw_counts(key, part):
    key = jax.random.fold_in(key, 12)
    first, second = jax.random.split(key)
    base = jax.random.randint(first, (N_LAT,), 1, PAIRS + 1)
    fullest = jax.random.randint(second, (), 0, N_LAT)
    return jnp.where(jnp.arange(N_LAT) == fullest, PAIRS, base).astype(jnp.int32)


def block_levels(rng, extent, pieces, least, top_value):
    gain, own = 1.0, jax.random.fold_in(rng, 6)
    for axis_at, shards_of in pieces:
        draws = jnp.exp(jax.random.uniform(jax.random.fold_in(own, axis_at), (shards_of,), jnp.float32, least / len(pieces), top_value / len(pieces)))
        gain = gain * jnp.repeat(draws, extent[axis_at] // shards_of).reshape([-1 if axis == axis_at else 1 for axis in range(len(extent))])
    return gain


def bell_draw(stream_key, shape, deviation, reach, cuts=(), kind=jnp.bfloat16):
    values = jax.random.normal(stream_key, shape, jnp.float32) * deviation
    if len(cuts) > 0:
        values = block_levels(stream_key, shape, cuts, -0.22, 0.18) * values
    return jnp.clip(values, min=-reach, max=reach).astype(kind)


def setup_inputs(seed: int = 0) -> dict:
    seeds = jax.random.split(jax.random.key(seed), 7)
    tokens = bell_draw(seeds[0], (ROWS, DIN), 1.0, 6.0, ((1, 8),))
    enc_weight = bell_draw(seeds[1], (DIN, LATENTS), DIN ** -0.5, 0.0625, ((0, 8), (1, 64)))
    enc_bias = jnp.clip(-1.5 + 2.0 * jax.random.uniform(seeds[2], (LATENTS,), jnp.float32) ** block_levels(seeds[2], (LATENTS,), ((0, 64),), -0.2, 0.2), -1.5, 0.5)
    dec_weight = bell_draw(seeds[3], (LATENTS, DIN), LATENTS ** -0.5, 0.03125, ((0, 64), (1, 8)))
    pairs = draw_pairs(jax.random.fold_in(seeds[6], 71), 0)
    counts = draw_counts(jax.random.fold_in(seeds[6], 71), 0)
    return {"tokens": tokens, "enc_weight": enc_weight, "enc_bias": enc_bias, "dec_weight": dec_weight, "pairs": pairs, "counts": counts}


PENALTY = 0.3
EPSILON = 1e-06

def shard_blocks(j, tokens, enc_weight, enc_bias, dec_weight, pairs, counts):
    codes = pairs[j]
    row_of = codes // LB
    lat_of = codes % LB
    valid = jnp.arange(PAIRS, dtype=jnp.int32) < counts[j]
    start = (j * (LB * BL)).astype(jnp.int32)
    enc_local = lax.dynamic_slice_in_dim(enc_weight, start, LB * BL, 1).reshape(DIN, LB, BL)
    dec_local = lax.dynamic_slice_in_dim(dec_weight, start, LB * BL, 0)
    bias_local = lax.dynamic_slice_in_dim(enc_bias, start, LB * BL, 0).reshape(LB, BL)
    x_sel = jnp.take(tokens.reshape(RBLK, BR, DIN), row_of, axis=0)
    enc_sel = jnp.take(enc_local, lat_of, axis=1)
    dec_sel = jnp.take(dec_local.reshape(LB, BL, DIN), lat_of, axis=0)
    pre = jnp.einsum('prd,dpl->prl', x_sel.astype(jnp.float32), enc_sel.astype(jnp.float32))
    pre = pre + jnp.take(bias_local, lat_of, axis=0)[:, None, :]
    acts = jnp.where(valid[:, None, None], jax.nn.softplus(pre), 0.0).astype(jnp.bfloat16)
    return (row_of, lat_of, valid, dec_local, x_sel, dec_sel, pre, acts)

def reference(tokens, enc_weight, enc_bias, dec_weight, pairs, counts):
    shard_ids = jnp.arange(N_LAT, dtype=jnp.int32)

    def add_shard(recon, j):
        row_of, lat_of, valid, dec_local, x_sel, dec_sel, pre, acts = shard_blocks(j, tokens, enc_weight, enc_bias, dec_weight, pairs, counts)
        contrib = jnp.einsum('prl,pld->prd', acts.astype(jnp.float32), dec_sel.astype(jnp.float32))
        place = ((row_of[:, None] == jnp.arange(RBLK, dtype=jnp.int32)[None, :]) & valid[:, None]).astype(jnp.float32)
        recon = recon + jnp.einsum('pg,prd->grd', place, contrib, precision=lax.Precision.HIGHEST)
        return (recon, None)
    recon, _ = lax.scan(add_shard, jnp.zeros((RBLK, BR, DIN), jnp.float32), shard_ids)
    error = (recon.reshape(ROWS, DIN) - tokens.astype(jnp.float32)).astype(jnp.bfloat16)
    error_blocks = error.reshape(RBLK, BR, DIN)

    def shard_grads(j):
        row_of, lat_of, valid, dec_local, x_sel, dec_sel, pre, acts = shard_blocks(j, tokens, enc_weight, enc_bias, dec_weight, pairs, counts)
        squares = jnp.square(dec_local.astype(jnp.float32))
        norm_a = jnp.sqrt(lax.optimization_barrier(jnp.sum(squares[:, :D], axis=1)) + EPSILON)
        norm_b = jnp.sqrt(lax.optimization_barrier(jnp.sum(squares[:, D:], axis=1)) + EPSILON)
        total_norm = (norm_a + norm_b).reshape(LB, BL)
        err_sel = jnp.take(error_blocks, row_of, axis=0)
        back = jnp.einsum('prd,pld->prl', err_sel.astype(jnp.float32), dec_sel.astype(jnp.float32))
        grad_act = jnp.where(valid[:, None, None], back + PENALTY * jnp.take(total_norm, lat_of, axis=0)[:, None, :], 0.0)
        grad_pre = (grad_act * jax.nn.sigmoid(pre)).astype(jnp.bfloat16)
        pick = ((lat_of[:, None] == jnp.arange(LB, dtype=jnp.int32)[None, :]) & valid[:, None]).astype(jnp.float32)
        enc_terms = jnp.einsum('prd,prl->pdl', x_sel.astype(jnp.float32), grad_pre.astype(jnp.float32))
        enc_local = jnp.einsum('pk,pdl->dkl', pick, enc_terms, precision=lax.Precision.HIGHEST).reshape(DIN, LB * BL)
        dec_terms = jnp.einsum('prl,prd->pld', acts.astype(jnp.float32), err_sel.astype(jnp.float32))
        dec_data = jnp.einsum('pk,pld->kld', pick, dec_terms, precision=lax.Precision.HIGHEST).reshape(LB * BL, DIN)
        act_sum = jnp.einsum('pk,pl->kl', pick, lax.optimization_barrier(jnp.sum(acts.astype(jnp.float32), axis=1)), precision=lax.Precision.HIGHEST).reshape(LB * BL)
        bias_local = jnp.einsum('pk,pl->kl', pick, lax.optimization_barrier(jnp.sum(grad_pre.astype(jnp.float32), axis=1)), precision=lax.Precision.HIGHEST).reshape(LB * BL)
        half_norm = jnp.concatenate([jnp.broadcast_to(norm_a[:, None], (LB * BL, D)), jnp.broadcast_to(norm_b[:, None], (LB * BL, D))], axis=1)
        dec_local_grad = dec_data + PENALTY * (act_sum[:, None] / half_norm) * dec_local.astype(jnp.float32)
        return (enc_local.astype(jnp.bfloat16), dec_local_grad.astype(jnp.bfloat16), bias_local)
    enc_stack, dec_stack, bias_stack = lax.map(shard_grads, shard_ids)
    enc_grad = enc_stack.transpose(1, 0, 2).reshape(DIN, LATENTS)
    dec_grad = dec_stack.reshape(LATENTS, DIN)
    bias_grad = bias_stack.reshape(LATENTS)
    return (error, enc_grad, dec_grad, bias_grad)
```

```python
import jax
import jax.numpy as jnp
from jax import lax
from jax.sharding import PartitionSpec as P

BR = 128
BL = 64
PENALTY = 0.3
EPSILON = 1e-06
EXTRA = 16

f32 = jnp.float32
bf16 = jnp.bfloat16


def body(tokens, enc_weight, enc_bias, dec_weight, pairs, counts):
    rows, width = tokens.shape
    local_lat = enc_weight.shape[1]
    nblk = local_lat // BL
    rblk = rows // BR
    slots = pairs.shape[1]
    n_lat = lax.axis_size("lat")
    n_tok = lax.axis_size("tok")
    tok = lax.axis_index("tok")
    half = tok * 2 // n_tok
    own = rows // n_tok
    share = rows // n_lat

    codes = pairs[0]
    valid = jnp.arange(slots, dtype=jnp.int32) < counts[0]
    g_own = tok * own // BR
    hit = valid[:, None] & (
        codes[:, None] == g_own * nblk + jnp.arange(local_lat, dtype=jnp.int32)[None, :] // BL
    )
    mask = jnp.any(hit, axis=0)[None, :]

    dec32 = dec_weight.astype(f32)
    squares = jnp.sum(dec32 * dec32, axis=1).astype(bf16)
    part = jnp.dot(tokens, enc_weight, preferred_element_type=f32).astype(bf16)
    packed = jnp.concatenate(
        [
            part.reshape(n_tok, own, local_lat),
            jnp.broadcast_to(squares[None, None, :], (n_tok, EXTRA, local_lat)),
        ],
        axis=1,
    )
    got = lax.all_to_all(packed, "tok", 0, 0, tiled=True)
    pre = jnp.sum(got[:, :own].astype(f32), axis=0) + enc_bias[None, :]
    sq = got[:, own].astype(f32)
    norm_a = jnp.sqrt(jnp.sum(sq[: n_tok // 2], axis=0) + EPSILON)
    norm_b = jnp.sqrt(jnp.sum(sq[n_tok // 2 :], axis=0) + EPSILON)
    total_norm = norm_a + norm_b
    own_norm = jnp.where(half == 0, norm_a, norm_b)

    acts_own = jnp.where(mask, jax.nn.softplus(pre), 0.0).astype(bf16)
    acts = lax.all_gather(acts_own, "tok", axis=0, tiled=True)

    recon = jnp.dot(acts, dec_weight, preferred_element_type=f32).astype(bf16)
    got = lax.all_to_all(recon.reshape(n_lat, share, width), "lat", 0, 0, tiled=True)
    x_own = lax.dynamic_slice_in_dim(tokens, lax.axis_index("lat") * share, share, 0)
    err_own = (jnp.sum(got.astype(f32), axis=0) - x_own.astype(f32)).astype(bf16)
    err = lax.all_to_all(
        jnp.broadcast_to(err_own[None], (n_lat, share, width)), "lat", 0, 0, tiled=True
    ).reshape(rows, width)

    back = lax.dot_general(
        err, dec_weight, (((1,), (1,)), ((), ())), preferred_element_type=f32
    ).astype(bf16)
    got = lax.all_to_all(back.reshape(n_tok, own, local_lat), "tok", 0, 0, tiled=True)
    grad_act = jnp.sum(got.astype(f32), axis=0) + PENALTY * total_norm[None, :]
    grad_own = jnp.where(mask, grad_act * jax.nn.sigmoid(pre), 0.0).astype(bf16)
    grad_pre = lax.all_gather(grad_own, "tok", axis=0, tiled=True)

    act_sum = jnp.sum(acts.astype(f32), axis=0)
    dec_data = lax.dot_general(acts, err, (((0,), (0,)), ((), ())), preferred_element_type=f32)
    dec_grad = dec_data + PENALTY * (act_sum / own_norm)[:, None] * dec32
    enc_grad = lax.dot_general(tokens, grad_pre, (((0,), (0,)), ((), ())), preferred_element_type=f32)
    bias_grad = jnp.sum(grad_pre.astype(f32), axis=0)
    return err_own, enc_grad.astype(bf16), dec_grad.astype(bf16), bias_grad


def solution(mesh):
    return jax.shard_map(
        body,
        mesh=mesh,
        in_specs=(
            P(None, "tok"),
            P("tok", "lat"),
            P("lat"),
            P("lat", "tok"),
            P("lat", None),
            P("lat"),
        ),
        out_specs=(P("lat", "tok"), P("tok", "lat"), P("lat", "tok"), P("lat")),
        check_vma=False,
    )
```

```python
import jax
import jax.numpy as jnp
from jax import lax
from jax.sharding import PartitionSpec as P

BR = 128
BL = 64
PENALTY = 0.3
EPSILON = 1e-06
EXTRA = 16

f32 = jnp.float32
bf16 = jnp.bfloat16


def lat_groups(n_lat, n_tok, first):
    side = round(n_lat**0.5)
    groups = []
    for tok in range(n_tok):
        inner = (tok % 2 == 0) == first
        for a in range(side):
            line = [a * side + b if inner else b * side + a for b in range(side)]
            groups.append([lat * n_tok + tok for lat in line])
    return groups


def exchange(x, groups):
    return lax.all_to_all(
        x, ("lat", "tok"), 0, 0, axis_index_groups=groups, tiled=True
    )


def body(tokens, enc_weight, enc_bias, dec_weight, pairs, counts):
    rows, width = tokens.shape
    local_lat = enc_weight.shape[1]
    nblk = local_lat // BL
    rblk = rows // BR
    slots = pairs.shape[1]
    n_lat = lax.axis_size("lat")
    n_tok = lax.axis_size("tok")
    tok = lax.axis_index("tok")
    half = tok * 2 // n_tok
    own = rows // n_tok
    share = rows // n_lat

    codes = pairs[0]
    valid = jnp.arange(slots, dtype=jnp.int32) < counts[0]
    g_own = tok * own // BR
    hit = valid[:, None] & (
        codes[:, None] == g_own * nblk + jnp.arange(local_lat, dtype=jnp.int32)[None, :] // BL
    )
    mask = jnp.any(hit, axis=0)[None, :]

    dec32 = dec_weight.astype(f32)
    squares = jnp.sum(dec32 * dec32, axis=1).astype(bf16)
    part = jnp.dot(tokens, enc_weight, preferred_element_type=f32).astype(bf16)
    packed = jnp.concatenate(
        [
            part.reshape(n_tok, own, local_lat),
            jnp.broadcast_to(squares[None, None, :], (n_tok, EXTRA, local_lat)),
        ],
        axis=1,
    )
    got = lax.all_to_all(packed, "tok", 0, 0, tiled=True)
    pre = jnp.sum(got[:, :own].astype(f32), axis=0) + enc_bias[None, :]
    sq = got[:, own].astype(f32)
    norm_a = jnp.sqrt(jnp.sum(sq[: n_tok // 2], axis=0) + EPSILON)
    norm_b = jnp.sqrt(jnp.sum(sq[n_tok // 2 :], axis=0) + EPSILON)
    total_norm = norm_a + norm_b
    own_norm = jnp.where(half == 0, norm_a, norm_b)

    acts_own = jnp.where(mask, jax.nn.softplus(pre), 0.0).astype(bf16)
    acts = lax.all_gather(acts_own, "tok", axis=0, tiled=True)

    side = round(n_lat**0.5)
    first = lat_groups(n_lat, n_tok, True)
    second = lat_groups(n_lat, n_tok, False)
    even = tok % 2 == 0

    def turn(v):
        v4 = v.reshape(side, side, share, v.shape[-1])
        return jnp.where(even, v4.transpose(1, 0, 2, 3), v4).reshape(v.shape)

    acts_t = turn(acts)
    recon = jnp.dot(acts_t, dec_weight, preferred_element_type=f32).astype(bf16)
    got = exchange(recon.reshape(side, side * share, width), first)
    line = jnp.sum(got.astype(f32), axis=0).astype(bf16)
    got = exchange(line.reshape(side, share, width), second)
    x_own = lax.dynamic_slice_in_dim(tokens, lax.axis_index("lat") * share, share, 0)
    err_own = (jnp.sum(got.astype(f32), axis=0) - x_own.astype(f32)).astype(bf16)
    line = exchange(jnp.broadcast_to(err_own[None], (side, share, width)), second)
    line = line.reshape(1, side * share, width)
    err = exchange(jnp.broadcast_to(line, (side, side * share, width)), first)
    err = err.reshape(rows, width)

    back = lax.dot_general(
        err, dec_weight, (((1,), (1,)), ((), ())), preferred_element_type=f32
    ).astype(bf16)
    back = turn(back)
    got = lax.all_to_all(back.reshape(n_tok, own, local_lat), "tok", 0, 0, tiled=True)
    grad_act = jnp.sum(got.astype(f32), axis=0) + PENALTY * total_norm[None, :]
    grad_own = jnp.where(mask, grad_act * jax.nn.sigmoid(pre), 0.0).astype(bf16)
    grad_pre = lax.all_gather(grad_own, "tok", axis=0, tiled=True)

    act_sum = jnp.sum(acts.astype(f32), axis=0)
    dec_data = lax.dot_general(acts_t, err, (((0,), (0,)), ((), ())), preferred_element_type=f32)
    dec_grad = dec_data + PENALTY * (act_sum / own_norm)[:, None] * dec32
    enc_grad = lax.dot_general(tokens, grad_pre, (((0,), (0,)), ((), ())), preferred_element_type=f32)
    bias_grad = jnp.sum(grad_pre.astype(f32), axis=0)
    return err_own, enc_grad.astype(bf16), dec_grad.astype(bf16), bias_grad


def solution(mesh):
    return jax.shard_map(
        body,
        mesh=mesh,
        in_specs=(
            P(None, "tok"),
            P("tok", "lat"),
            P("lat"),
            P("lat", "tok"),
            P("lat", None),
            P("lat"),
        ),
        out_specs=(P("lat", "tok"), P("tok", "lat"), P("lat", "tok"), P("lat")),
        check_vma=False,
    )
```

```python
import jax
import jax.numpy as jnp
from jax import lax
from jax.sharding import PartitionSpec as P

BR = 128
BL = 64
PENALTY = 0.3
EPSILON = 1e-06
EXTRA = 8

f32 = jnp.float32
bf16 = jnp.bfloat16


def lat_groups(n_lat, n_tok):
    side = round(n_lat**0.5)
    quads = side // 2
    big, small = [], []
    for tok in range(n_tok):
        swap = tok % 2 == 1

        def device(a, p, b):
            pair = 2 * a + p
            lat = b * side + pair if swap else pair * side + b
            return lat * n_tok + tok

        for a in range(quads):
            big.append([device(a, p, b) for p in range(2) for b in range(side)])
        for p in range(2):
            for b in range(side):
                small.append([device(a, p, b) for a in range(quads)])
    return big, small


def exchange(x, axis, groups):
    return lax.all_to_all(x, axis, 0, 0, axis_index_groups=groups, tiled=True)


def body(tokens, enc_weight, enc_bias, dec_weight, pairs, counts):
    rows, width = tokens.shape
    local_lat = enc_weight.shape[1]
    nblk = local_lat // BL
    slots = pairs.shape[1]
    n_lat = lax.axis_size("lat")
    n_tok = lax.axis_size("tok")
    lat = lax.axis_index("lat")
    tok = lax.axis_index("tok")
    half = tok * 2 // n_tok
    own = rows // n_tok
    share = rows // n_lat
    side = round(n_lat**0.5)
    quads = side // 2
    n_x = n_tok // 2
    even = tok % 2 == 0
    both = ("lat", "tok")
    big, small = lat_groups(n_lat, n_tok)
    x_groups = [[2 * x + c for x in range(n_x)] for c in range(2)]
    c_groups = [[2 * x, 2 * x + 1] for x in range(n_x)]

    def gather_tok(v):
        spread = jnp.broadcast_to(v[None], (n_x,) + v.shape)
        got = exchange(spread, "tok", x_groups)
        return lax.all_gather(
            got.reshape(n_x * own, local_lat), "tok", axis_index_groups=c_groups, axis=0, tiled=True
        )

    codes = pairs[0]
    valid = jnp.arange(slots, dtype=jnp.int32) < counts[0]
    g_own = tok * own // BR
    hit = valid[:, None] & (
        codes[:, None] == g_own * nblk + jnp.arange(local_lat, dtype=jnp.int32)[None, :] // BL
    )
    mask = jnp.any(hit, axis=0)[None, :]

    part = jnp.dot(tokens, enc_weight, preferred_element_type=f32).astype(bf16)
    got = exchange(part.reshape(n_tok, own, local_lat), "tok", None)
    pre = jnp.sum(got.astype(f32), axis=0) + enc_bias[None, :]
    acts_own = jnp.where(mask, jax.nn.softplus(pre), 0.0).astype(bf16)
    acts = gather_tok(acts_own)

    acts_even = acts.reshape(2, n_x, side, share, local_lat).transpose(0, 2, 1, 3, 4)
    acts_odd = acts.reshape(2, n_x, quads, 2, share, local_lat).transpose(3, 1, 0, 2, 4, 5)
    acts_t = jnp.where(
        even, acts_even.reshape(rows, local_lat), acts_odd.reshape(rows, local_lat)
    )

    recon = jnp.dot(acts_t, dec_weight, preferred_element_type=f32).astype(bf16)
    got = exchange(recon.reshape(2 * side, quads * share, width), both, big)
    line = jnp.sum(got.astype(f32), axis=0).astype(bf16)
    got = exchange(jnp.broadcast_to(line[None], (quads,) + line.shape), both, small)
    y, z = lat // side, lat % side
    x_rows = []
    for a in range(quads):
        at = jnp.where(even, (2 * a + y % 2) * side + z, y * side + 2 * a + z % 2)
        x_rows.append(lax.dynamic_slice_in_dim(tokens, at * share, share, 0))
    x_line = jnp.concatenate(x_rows, axis=0)
    err_line = (jnp.sum(got.astype(f32), axis=0) - x_line.astype(f32)).astype(bf16)
    a_own = jnp.where(even, y, z) // 2
    err_own = lax.dynamic_slice_in_dim(err_line, a_own * share, share, 0)
    err = exchange(jnp.broadcast_to(err_line[None], (2 * side,) + err_line.shape), both, big)
    err = err.reshape(rows, width)

    back = lax.dot_general(
        err, dec_weight, (((1,), (1,)), ((), ())), preferred_element_type=f32
    ).astype(bf16)
    back_even = back.reshape(2, side, quads, share, local_lat).transpose(2, 0, 1, 3, 4)
    back_odd = back.reshape(2, side, quads, share, local_lat).transpose(1, 2, 0, 3, 4)
    shape = (n_tok, own, local_lat)
    back = jnp.where(even, back_even.reshape(shape), back_odd.reshape(shape))
    dec32 = dec_weight.astype(f32)
    squares = jnp.sum(dec32 * dec32, axis=1).astype(bf16)
    packed = jnp.concatenate(
        [back, jnp.broadcast_to(squares[None, None, :], (n_tok, EXTRA, local_lat))], axis=1
    )
    got = exchange(packed, "tok", None)
    sq = got[:, own].astype(f32)
    norm_a = jnp.sqrt(jnp.sum(sq[: n_tok // 2], axis=0) + EPSILON)
    norm_b = jnp.sqrt(jnp.sum(sq[n_tok // 2 :], axis=0) + EPSILON)
    own_norm = jnp.where(half == 0, norm_a, norm_b)
    grad_act = jnp.sum(got[:, :own].astype(f32), axis=0) + PENALTY * (norm_a + norm_b)[None, :]
    grad_own = jnp.where(mask, grad_act * jax.nn.sigmoid(pre), 0.0).astype(bf16)
    grad_pre = gather_tok(grad_own)

    act_sum = jnp.sum(acts.astype(f32), axis=0)
    dec_data = lax.dot_general(acts_t, err, (((0,), (0,)), ((), ())), preferred_element_type=f32)
    dec_grad = dec_data + PENALTY * (act_sum / own_norm)[:, None] * dec32
    tokens_t = tokens.reshape(n_x, 2, own, width).transpose(1, 0, 2, 3).reshape(rows, width)
    enc_grad = lax.dot_general(
        tokens_t, grad_pre, (((0,), (0,)), ((), ())), preferred_element_type=f32
    )
    bias_grad = jnp.sum(grad_pre.astype(f32), axis=0)
    return err_own, enc_grad.astype(bf16), dec_grad.astype(bf16), bias_grad


def solution(mesh):
    return jax.shard_map(
        body,
        mesh=mesh,
        in_specs=(
            P(None, "tok"),
            P("tok", "lat"),
            P("lat"),
            P("lat", "tok"),
            P("lat", None),
            P("lat"),
        ),
        out_specs=(P("lat", "tok"), P("tok", "lat"), P("lat", "tok"), P("lat")),
        check_vma=False,
    )
```

```python
import jax
import jax.numpy as jnp
from jax import lax
from jax.experimental import pallas as pl
from jax.experimental.pallas import tpu as pltpu
from jax.sharding import PartitionSpec as P

BR = 128
BL = 64
PENALTY = 0.3
EPSILON = 1e-06
EXTRA = 8

f32 = jnp.float32
bf16 = jnp.bfloat16


def lat_groups(n_lat, n_tok):
    side = round(n_lat**0.5)
    quads = side // 2
    big, near, far = [], [], []
    for tok in range(n_tok):
        swap = tok % 2 == 1

        def device(a, p, b):
            pair = 2 * a + p
            lat = b * side + pair if swap else pair * side + b
            return lat * n_tok + tok

        for a in range(quads):
            big.append([device(a, p, b) for p in range(2) for b in range(side)])
        for p in range(2):
            for b in range(side):
                four = [device(a, p, b) for a in range(quads)]
                near += [four[:2], four[2:]]
                far += [four[1:3], [four[0], four[3]]]
    return big, near, far


def exchange(x, axis, groups):
    return lax.all_to_all(x, axis, 0, 0, axis_index_groups=groups, tiled=True)


def head_kernel(x_ref, w_ref, out_ref, total):
    step = pl.program_id(0)
    part = jnp.dot(x_ref[...], w_ref[...], preferred_element_type=f32)

    @pl.when(step == 0)
    def _():
        total[...] = part

    @pl.when(step > 0)
    def _():
        total[...] += part

    @pl.when(step == pl.num_programs(0) - 1)
    def _():
        out_ref[...] = total[...].astype(bf16)


def head(x, w):
    rows, depth = x.shape
    cols = w.shape[1]
    step = depth // 3
    return pl.pallas_call(
        head_kernel,
        grid=(3,),
        in_specs=[
            pl.BlockSpec((rows, step), lambda i: (0, i)),
            pl.BlockSpec((step, cols), lambda i: (i, 0)),
        ],
        out_specs=pl.BlockSpec((rows, cols), lambda i: (0, 0)),
        out_shape=jax.ShapeDtypeStruct((rows, cols), bf16),
        scratch_shapes=[pltpu.VMEM((rows, cols), f32)],
        compiler_params=pltpu.CompilerParams(vmem_limit_bytes=24 * 2**20),
    )(x, w)


def tail_kernel(x_ref, g_ref, out_ref, bias_ref):
    out_ref[...] = jnp.dot(x_ref[...], g_ref[...], preferred_element_type=f32).astype(bf16)

    @pl.when(pl.program_id(0) == 0)
    def _():
        ones = jnp.ones((8, g_ref.shape[0]), bf16)
        bias_ref[...] = jnp.dot(ones, g_ref[...], preferred_element_type=f32)


def tail(x_t, g):
    depth, rows = x_t.shape
    cols = g.shape[1]
    step = depth // 3
    enc, bias = pl.pallas_call(
        tail_kernel,
        grid=(3,),
        in_specs=[
            pl.BlockSpec((step, rows), lambda i: (i, 0)),
            pl.BlockSpec((rows, cols), lambda i: (0, 0)),
        ],
        out_specs=[
            pl.BlockSpec((step, cols), lambda i: (i, 0)),
            pl.BlockSpec((8, cols), lambda i: (0, 0)),
        ],
        out_shape=[
            jax.ShapeDtypeStruct((depth, cols), bf16),
            jax.ShapeDtypeStruct((8, cols), f32),
        ],
        compiler_params=pltpu.CompilerParams(vmem_limit_bytes=24 * 2**20),
    )(x_t, g)
    return enc, bias[0]


def body(tokens, enc_weight, enc_bias, dec_weight, pairs, counts):
    rows, width = tokens.shape
    local_lat = enc_weight.shape[1]
    nblk = local_lat // BL
    slots = pairs.shape[1]
    n_lat = lax.axis_size("lat")
    n_tok = lax.axis_size("tok")
    lat = lax.axis_index("lat")
    tok = lax.axis_index("tok")
    half = tok * 2 // n_tok
    own = rows // n_tok
    share = rows // n_lat
    side = round(n_lat**0.5)
    quads = side // 2
    n_x = n_tok // 2
    even = tok % 2 == 0
    both = ("lat", "tok")
    big, near, far = lat_groups(n_lat, n_tok)
    x_groups = [[2 * x + c for x in range(n_x)] for c in range(2)]
    c_groups = [[2 * x, 2 * x + 1] for x in range(n_x)]

    def gather_tok(v):
        spread = jnp.broadcast_to(v[None], (n_x,) + v.shape)
        got = exchange(spread, "tok", x_groups)
        return lax.all_gather(
            got.reshape(-1, local_lat), "tok", axis_index_groups=c_groups, axis=0, tiled=True
        )

    codes = pairs[0]
    valid = jnp.arange(slots, dtype=jnp.int32) < counts[0]
    g_own = tok * own // BR
    hit = valid[:, None] & (
        codes[:, None] == g_own * nblk + jnp.arange(local_lat, dtype=jnp.int32)[None, :] // BL
    )
    mask = jnp.any(hit, axis=0)[None, :]

    dec32 = dec_weight.astype(f32)
    squares = jnp.sum(dec32 * dec32, axis=1).astype(bf16)
    part = head(tokens, enc_weight)
    got = exchange(part.reshape(n_tok, own, local_lat), "tok", None)
    pre = jnp.sum(got.astype(f32), axis=0) + enc_bias[None, :]
    acts_own = jnp.where(mask, jax.nn.softplus(pre), 0.0).astype(bf16)
    extra = jnp.broadcast_to(squares[None, :], (EXTRA, local_lat))
    got = gather_tok(jnp.concatenate([acts_own, extra], axis=0))
    got = got.reshape(2, n_x, own + EXTRA, local_lat)
    acts = got[:, :, :own]
    sq = got[:, :, own].astype(f32)
    norm_a = jnp.sqrt(jnp.sum(sq[:, : n_x // 2], axis=(0, 1)) + EPSILON)
    norm_b = jnp.sqrt(jnp.sum(sq[:, n_x // 2 :], axis=(0, 1)) + EPSILON)
    own_norm = jnp.where(half == 0, norm_a, norm_b)

    acts_even = acts.reshape(2, n_x, side, share, local_lat).transpose(0, 2, 1, 3, 4)
    acts_odd = acts.reshape(2, n_x, quads, 2, share, local_lat).transpose(3, 1, 0, 2, 4, 5)
    acts_t = jnp.where(
        even, acts_even.reshape(rows, local_lat), acts_odd.reshape(rows, local_lat)
    )

    recon = jnp.dot(acts_t, dec_weight, preferred_element_type=f32).astype(bf16)
    got = exchange(recon.reshape(2 * side, quads * share, width), both, big)
    line = jnp.sum(got.astype(f32), axis=0).astype(bf16)
    for groups in (near, far):
        two = lax.all_gather(line, both, axis_index_groups=groups, axis=0)
        total = jnp.sum(two.astype(f32), axis=0)
        line = total.astype(bf16)
    y, z = lat // side, lat % side
    x_rows = []
    for a in range(quads):
        at = jnp.where(even, (2 * a + y % 2) * side + z, y * side + 2 * a + z % 2)
        x_rows.append(lax.dynamic_slice_in_dim(tokens, at * share, share, 0))
    x_line = jnp.concatenate(x_rows, axis=0)
    err_line = (total - x_line.astype(f32)).astype(bf16)
    a_own = jnp.where(even, y, z) // 2
    err_own = lax.dynamic_slice_in_dim(err_line, a_own * share, share, 0)
    err = exchange(jnp.broadcast_to(err_line[None], (2 * side,) + err_line.shape), both, big)
    err = err.reshape(rows, width)

    back = lax.dot_general(
        err, dec_weight, (((1,), (1,)), ((), ())), preferred_element_type=f32
    ).astype(bf16)
    back_even = back.reshape(2, side, quads, share, local_lat).transpose(2, 0, 1, 3, 4)
    back_odd = back.reshape(2, side, quads, share, local_lat).transpose(1, 2, 0, 3, 4)
    shape = (n_tok, own, local_lat)
    back = jnp.where(even, back_even.reshape(shape), back_odd.reshape(shape))
    got = exchange(back, "tok", None)
    grad_act = jnp.sum(got.astype(f32), axis=0) + PENALTY * (norm_a + norm_b)[None, :]
    grad_own = jnp.where(mask, grad_act * jax.nn.sigmoid(pre), 0.0).astype(bf16)
    grad_pre = gather_tok(grad_own)

    act_sum = jnp.sum(acts_t.astype(f32), axis=0)
    dec_data = lax.dot_general(acts_t, err, (((0,), (0,)), ((), ())), preferred_element_type=f32)
    dec_grad = dec_data + PENALTY * (act_sum / own_norm)[:, None] * dec32
    tokens_t = tokens.reshape(n_x, 2, own, width).transpose(3, 1, 0, 2).reshape(width, rows)
    enc_grad, bias_grad = tail(tokens_t, grad_pre)
    return err_own, enc_grad, dec_grad.astype(bf16), bias_grad


def solution(mesh):
    return jax.shard_map(
        body,
        mesh=mesh,
        in_specs=(
            P(None, "tok"),
            P("tok", "lat"),
            P("lat"),
            P("lat", "tok"),
            P("lat", None),
            P("lat"),
        ),
        out_specs=(P("lat", "tok"), P("tok", "lat"), P("lat", "tok"), P("lat")),
        check_vma=False,
    )
```

```python
import jax
import jax.numpy as jnp
from jax import lax
from jax.experimental import pallas as pl
from jax.experimental.pallas import tpu as pltpu
from jax.sharding import PartitionSpec as P

BR = 128
BL = 64
PENALTY = 0.3
EPSILON = 1e-06
EXTRA = 8

f32 = jnp.float32
bf16 = jnp.bfloat16


def lat_groups(n_lat, n_tok):
    side = round(n_lat**0.5)
    quads = side // 2
    line, near, far, swap = [], [], [], []
    for tok in range(n_tok):

        def device(pair, b):
            lat = b * side + pair if tok % 2 == 1 else pair * side + b
            return lat * n_tok + tok

        for pair in range(side):
            line.append([device(pair, b) for b in range(side)])
            swap += [(device(pair, b), device(pair ^ 1, b)) for b in range(side)]
        for p in range(2):
            for b in range(side):
                four = [device(2 * a + p, b) for a in range(quads)]
                near += [four[:2], four[2:]]
                far += [four[1:3], [four[0], four[3]]]
    return line, near, far, swap


def exchange(x, axis, groups):
    return lax.all_to_all(x, axis, 0, 0, axis_index_groups=groups, tiled=True)


def tail_kernel(x_ref, g_ref, out_ref, bias_ref):
    out_ref[...] = jnp.dot(x_ref[...], g_ref[...], preferred_element_type=f32).astype(bf16)

    @pl.when(pl.program_id(0) == 0)
    def _():
        ones = jnp.ones((8, g_ref.shape[0]), bf16)
        bias_ref[...] = jnp.dot(ones, g_ref[...], preferred_element_type=f32)[0]


def tail(x_t, g):
    depth, rows = x_t.shape
    cols = g.shape[1]
    step = depth // 3
    return pl.pallas_call(
        tail_kernel,
        grid=(3,),
        in_specs=[
            pl.BlockSpec((step, rows), lambda i: (i, 0)),
            pl.BlockSpec((rows, cols), lambda i: (0, 0)),
        ],
        out_specs=[
            pl.BlockSpec((step, cols), lambda i: (i, 0)),
            pl.BlockSpec((cols,), lambda i: (0,)),
        ],
        out_shape=[
            jax.ShapeDtypeStruct((depth, cols), bf16),
            jax.ShapeDtypeStruct((cols,), f32),
        ],
        compiler_params=pltpu.CompilerParams(vmem_limit_bytes=24 * 2**20),
    )(x_t, g)


def body(tokens, enc_weight, enc_bias, dec_weight, pairs, counts):
    rows, width = tokens.shape
    local_lat = enc_weight.shape[1]
    nblk = local_lat // BL
    slots = pairs.shape[1]
    n_lat = lax.axis_size("lat")
    n_tok = lax.axis_size("tok")
    lat = lax.axis_index("lat")
    tok = lax.axis_index("tok")
    half = tok * 2 // n_tok
    own = rows // n_tok
    share = rows // n_lat
    side = round(n_lat**0.5)
    quads = side // 2
    n_x = n_tok // 2
    even = tok % 2 == 0
    both = ("lat", "tok")
    line_groups, near, far, swap = lat_groups(n_lat, n_tok)
    x_groups = [[2 * x + c for x in range(n_x)] for c in range(2)]
    c_groups = [[2 * x, 2 * x + 1] for x in range(n_x)]

    def gather_tok(v):
        spread = jnp.broadcast_to(v[None], (n_x,) + v.shape)
        got = exchange(spread, "tok", x_groups)
        return lax.all_gather(
            got.reshape(-1, local_lat), "tok", axis_index_groups=c_groups, axis=0, tiled=True
        )

    codes = pairs[0]
    valid = jnp.arange(slots, dtype=jnp.int32) < counts[0]
    g_own = tok * own // BR
    hit = valid[:, None] & (
        codes[:, None] == g_own * nblk + jnp.arange(local_lat, dtype=jnp.int32)[None, :] // BL
    )
    mask = jnp.any(hit, axis=0)[None, :]

    dec32 = dec_weight.astype(f32)
    squares = jnp.sum(dec32 * dec32, axis=1).astype(bf16)
    part = jnp.dot(tokens, enc_weight, preferred_element_type=f32).astype(bf16)
    part, squares = lax.optimization_barrier((part, squares))
    got = exchange(part.reshape(n_tok, own, local_lat), "tok", None)
    pre = jnp.sum(got.astype(f32), axis=0) + enc_bias[None, :]
    acts_own = jnp.where(mask, jax.nn.softplus(pre), 0.0).astype(bf16)
    extra = jnp.broadcast_to(squares[None, :], (EXTRA, local_lat))
    got = gather_tok(jnp.concatenate([acts_own, extra], axis=0))
    got = got.reshape(2, n_x, own + EXTRA, local_lat)
    acts = got[:, :, :own]
    sq = got[:, :, own].astype(f32)
    norm_a = jnp.sqrt(jnp.sum(sq[:, : n_x // 2], axis=(0, 1)) + EPSILON)
    norm_b = jnp.sqrt(jnp.sum(sq[:, n_x // 2 :], axis=(0, 1)) + EPSILON)
    own_norm = jnp.where(half == 0, norm_a, norm_b)

    acts_even = acts.reshape(2, n_x, side, share, local_lat).transpose(0, 2, 1, 3, 4)
    acts_odd = acts.reshape(2, n_x, quads, 2, share, local_lat).transpose(3, 1, 0, 2, 4, 5)
    halves = jnp.where(
        even,
        acts_even.reshape(2, rows // 2, local_lat),
        acts_odd.reshape(2, rows // 2, local_lat),
    )
    y, z = lat // side, lat % side
    low = jnp.where(even, y, z) % 2 == 0
    acts_kept = jnp.where(low, halves[0], halves[1])
    acts_sent = jnp.where(low, halves[1], halves[0])

    sent = jnp.dot(acts_sent, dec_weight, preferred_element_type=f32).astype(bf16)
    came = lax.ppermute(sent, both, swap)
    kept = jnp.dot(acts_kept, dec_weight, preferred_element_type=f32)
    recon = (kept + came.astype(f32)).astype(bf16)
    got = exchange(recon.reshape(side, quads * share, width), both, line_groups)
    line = jnp.sum(got.astype(f32), axis=0).astype(bf16)
    for groups in (near, far):
        two = lax.all_gather(line, both, axis_index_groups=groups, axis=0)
        total = jnp.sum(two.astype(f32), axis=0)
        line = total.astype(bf16)
    x_rows = []
    for a in range(quads):
        at = jnp.where(even, (2 * a + y % 2) * side + z, y * side + 2 * a + z % 2)
        x_rows.append(lax.dynamic_slice_in_dim(tokens, at * share, share, 0))
    x_line = jnp.concatenate(x_rows, axis=0)
    err_line = (total - x_line.astype(f32)).astype(bf16)
    a_own = jnp.where(even, y, z) // 2
    err_own = lax.dynamic_slice_in_dim(err_line, a_own * share, share, 0)
    err_kept = exchange(
        jnp.broadcast_to(err_line[None], (side,) + err_line.shape), both, line_groups
    ).reshape(rows // 2, width)
    err_came = lax.ppermute(err_kept, both, swap)

    def back_of(e):
        return lax.dot_general(
            e, dec_weight, (((1,), (1,)), ((), ())), preferred_element_type=f32
        ).astype(bf16)

    back_kept, back_came = back_of(err_kept), back_of(err_came)
    back = jnp.stack(
        [jnp.where(low, back_kept, back_came), jnp.where(low, back_came, back_kept)]
    ).reshape(2, side, quads, share, local_lat)
    shape = (n_tok, own, local_lat)
    back = jnp.where(
        even,
        back.transpose(2, 0, 1, 3, 4).reshape(shape),
        back.transpose(1, 2, 0, 3, 4).reshape(shape),
    )
    got = exchange(back, "tok", None)
    grad_act = jnp.sum(got.astype(f32), axis=0) + PENALTY * (norm_a + norm_b)[None, :]
    grad_own = jnp.where(mask, grad_act * jax.nn.sigmoid(pre), 0.0).astype(bf16)
    grad_pre = gather_tok(grad_own)

    acts_t = jnp.concatenate([acts_kept, acts_sent], axis=0)
    err = jnp.concatenate([err_kept, err_came], axis=0)
    act_sum = jnp.sum(acts_t.astype(f32), axis=0)
    dec_data = lax.dot_general(acts_t, err, (((0,), (0,)), ((), ())), preferred_element_type=f32)
    dec_grad = dec_data + PENALTY * (act_sum / own_norm)[:, None] * dec32
    tokens_t = tokens.reshape(n_x, 2, own, width).transpose(3, 1, 0, 2).reshape(width, rows)
    enc_grad, bias_grad = tail(tokens_t, grad_pre)
    return err_own, enc_grad, dec_grad.astype(bf16), bias_grad


def solution(mesh):
    return jax.shard_map(
        body,
        mesh=mesh,
        in_specs=(
            P(None, "tok"),
            P("tok", "lat"),
            P("lat"),
            P("lat", "tok"),
            P("lat", None),
            P("lat"),
        ),
        out_specs=(P("lat", "tok"), P("tok", "lat"), P("lat", "tok"), P("lat")),
        check_vma=False,
    )
```

```python
import jax
import jax.numpy as jnp
from jax import lax
from jax.experimental import pallas as pl
from jax.experimental.pallas import tpu as pltpu
from jax.sharding import PartitionSpec as P

BR = 128
BL = 64
PENALTY = 0.3
EPSILON = 1e-06
EXTRA = 8

f32 = jnp.float32
bf16 = jnp.bfloat16


def lat_groups(n_lat, n_tok):
    side = round(n_lat**0.5)
    quads = side // 2
    big, near, far = [], [], []
    for tok in range(n_tok):

        def device(a, p, b):
            pair = 2 * a + p
            lat = b * side + pair if tok % 2 == 1 else pair * side + b
            return lat * n_tok + tok

        for a in range(quads):
            big.append([device(a, p, b) for p in range(2) for b in range(side)])
        for p in range(2):
            for b in range(side):
                four = [device(a, p, b) for a in range(quads)]
                near += [four[:2], four[2:]]
                far += [four[1:3], [four[0], four[3]]]
    return big, near, far


def exchange(x, axis, groups):
    return lax.all_to_all(x, axis, 0, 0, axis_index_groups=groups, tiled=True)


def tail_kernel(x_ref, g_ref, out_ref, bias_ref):
    out_ref[...] = jnp.dot(x_ref[...], g_ref[...], preferred_element_type=f32).astype(bf16)

    @pl.when(pl.program_id(0) == 0)
    def _():
        ones = jnp.ones((8, g_ref.shape[0]), bf16)
        bias_ref[...] = jnp.dot(ones, g_ref[...], preferred_element_type=f32)[0]


def tail(x_t, g):
    depth, rows = x_t.shape
    cols = g.shape[1]
    step = depth // 3
    return pl.pallas_call(
        tail_kernel,
        grid=(3,),
        in_specs=[
            pl.BlockSpec((step, rows), lambda i: (i, 0)),
            pl.BlockSpec((rows, cols), lambda i: (0, 0)),
        ],
        out_specs=[
            pl.BlockSpec((step, cols), lambda i: (i, 0)),
            pl.BlockSpec((cols,), lambda i: (0,)),
        ],
        out_shape=[
            jax.ShapeDtypeStruct((depth, cols), bf16),
            jax.ShapeDtypeStruct((cols,), f32),
        ],
        compiler_params=pltpu.CompilerParams(vmem_limit_bytes=24 * 2**20),
    )(x_t, g)


def body(tokens, enc_weight, enc_bias, dec_weight, pairs, counts):
    rows, width = tokens.shape
    local_lat = enc_weight.shape[1]
    nblk = local_lat // BL
    slots = pairs.shape[1]
    n_lat = lax.axis_size("lat")
    n_tok = lax.axis_size("tok")
    lat = lax.axis_index("lat")
    tok = lax.axis_index("tok")
    own = rows // n_tok
    share = rows // n_lat
    side = round(n_lat**0.5)
    n_x = n_tok // 2
    x, core = tok // 2, tok % 2
    y, z = lat // side, lat % side
    both = ("lat", "tok")
    big, near, far = lat_groups(n_lat, n_tok)
    chunks = 2 * side
    part_rows = n_x * own
    chunk = part_rows // chunks
    x_groups = [[2 * i + c for i in range(n_x)] for c in range(2)]
    c_groups = [[2 * i, 2 * i + 1] for i in range(n_x)]

    def swap(v):
        return lax.ppermute(v, "tok", [(t, t ^ 1) for t in range(n_tok)])

    def gather_x(v):
        spread = jnp.broadcast_to(v[None], (n_x,) + v.shape)
        return exchange(spread, "tok", x_groups)

    def chunk_tokens(c):
        at = jnp.where(c == 0, y % 2 * side + z, z % 2 * side + y) * chunk
        at = (2 * (at // own) + c) * own + at % own
        return lax.dynamic_slice_in_dim(tokens, at, chunk, 0)

    codes = pairs[0]
    valid = jnp.arange(slots, dtype=jnp.int32) < counts[0]
    g_own = tok * own // BR
    hit = valid[:, None] & (
        codes[:, None] == g_own * nblk + jnp.arange(local_lat, dtype=jnp.int32)[None, :] // BL
    )
    mask = jnp.any(hit, axis=0)[None, :]

    dec32 = dec_weight.astype(f32)
    squares = jnp.sum(dec32 * dec32, axis=1)
    part = jnp.dot(tokens, enc_weight, preferred_element_type=f32).astype(bf16)
    part, squares = lax.optimization_barrier((part, squares))
    dec_came = swap(dec_weight)
    x_line = jnp.concatenate([chunk_tokens(core), swap(chunk_tokens(1 - core))], axis=1)
    dec_both = jnp.concatenate([dec_weight, dec_came], axis=1)
    came32 = dec_came.astype(f32)
    squares = (squares + jnp.sum(came32 * came32, axis=1)).astype(bf16)

    got = exchange(part.reshape(n_tok, own, local_lat), "tok", None)
    pre = jnp.sum(got.astype(f32), axis=0) + enc_bias[None, :]
    acts_own = jnp.where(mask, jax.nn.softplus(pre), 0.0).astype(bf16)
    extra = jnp.broadcast_to(squares[None, :], (EXTRA, local_lat))
    got = gather_x(jnp.concatenate([acts_own, extra], axis=0))
    acts = got[:, :own].reshape(part_rows, local_lat)
    sq = got[:, own].astype(f32)
    norm_a = jnp.sqrt(jnp.sum(sq[: n_x // 2], axis=0) + EPSILON)
    norm_b = jnp.sqrt(jnp.sum(sq[n_x // 2 :], axis=0) + EPSILON)
    own_norm = jnp.where(x < n_x // 2, norm_a, norm_b)

    recon = jnp.dot(acts, dec_both, preferred_element_type=f32).astype(bf16)
    got = exchange(recon.reshape(chunks, chunk, 2 * width), both, big)
    line = jnp.sum(got.astype(f32), axis=0).astype(bf16)
    for groups in (near, far):
        two = lax.all_gather(line, both, axis_index_groups=groups, axis=0)
        total = jnp.sum(two.astype(f32), axis=0)
        line = total.astype(bf16)
    err_line = (total - x_line.astype(f32)).astype(bf16)
    spread = jnp.broadcast_to(err_line[None], (chunks,) + err_line.shape)
    err = exchange(spread, both, big).reshape(part_rows, 2 * width)

    back = lax.dot_general(
        err, dec_both, (((1,), (1,)), ((), ())), preferred_element_type=f32
    ).astype(bf16)
    got = exchange(back.reshape(n_x, own, local_lat), "tok", x_groups)
    grad_act = jnp.sum(got.astype(f32), axis=0) + PENALTY * (norm_a + norm_b)[None, :]
    grad_own = jnp.where(mask, grad_act * jax.nn.sigmoid(pre), 0.0).astype(bf16)
    grad_pre = lax.all_gather(
        gather_x(grad_own).reshape(part_rows, local_lat),
        "tok",
        axis_index_groups=c_groups,
        axis=0,
        tiled=True,
    )

    acts_all = jnp.concatenate([acts, swap(acts)], axis=0)
    err_mine, err_came = err[:, :width], swap(err[:, width:])
    err_all = jnp.concatenate([err_mine, err_came], axis=0)
    at = jnp.where(y % 2 == core, 0, part_rows) + y // 2 * own + z * share
    err_own = lax.dynamic_slice_in_dim(err_all, at, share, 0)
    act_sum = jnp.sum(acts_all.astype(f32), axis=0)
    dec_data = lax.dot_general(
        acts_all, err_all, (((0,), (0,)), ((), ())), preferred_element_type=f32
    )
    dec_grad = dec_data + PENALTY * (act_sum / own_norm)[:, None] * dec32
    tokens_t = tokens.reshape(n_x, 2, own, width).transpose(3, 1, 0, 2).reshape(width, rows)
    enc_grad, bias_grad = tail(tokens_t, grad_pre)
    return err_own, enc_grad, dec_grad.astype(bf16), bias_grad


def solution(mesh):
    return jax.shard_map(
        body,
        mesh=mesh,
        in_specs=(
            P(None, "tok"),
            P("tok", "lat"),
            P("lat"),
            P("lat", "tok"),
            P("lat", None),
            P("lat"),
        ),
        out_specs=(P("lat", "tok"), P("tok", "lat"), P("lat", "tok"), P("lat")),
        check_vma=False,
    )
```

```python
import jax
import jax.numpy as jnp
from jax import lax
from jax.experimental import pallas as pl
from jax.experimental.pallas import tpu as pltpu
from jax.sharding import PartitionSpec as P

BR = 128
BL = 64
PENALTY = 0.3
EPSILON = 1e-06
EXTRA = 8

f32 = jnp.float32
bf16 = jnp.bfloat16


def lat_groups(n_lat, n_tok):
    side = round(n_lat**0.5)
    quads = side // 2
    big, near, far = [], [], []
    for tok in range(n_tok):
        swap = tok % 2 == 1

        def device(a, p, b):
            pair = 2 * a + p
            lat = b * side + pair if swap else pair * side + b
            return lat * n_tok + tok

        for a in range(quads):
            big.append([device(a, p, b) for p in range(2) for b in range(side)])
        for p in range(2):
            for b in range(side):
                four = [device(a, p, b) for a in range(quads)]
                near += [four[:2], four[2:]]
                far += [four[1:3], [four[0], four[3]]]
    return big, near, far


def exchange(x, axis, groups):
    return lax.all_to_all(x, axis, 0, 0, axis_index_groups=groups, tiled=True)


def tail_kernel(x_ref, g_ref, out_ref, bias_ref):
    out_ref[...] = jnp.dot(x_ref[...], g_ref[...], preferred_element_type=f32).astype(bf16)

    @pl.when(pl.program_id(0) == 0)
    def _():
        ones = jnp.ones((8, g_ref.shape[0]), bf16)
        bias_ref[...] = jnp.dot(ones, g_ref[...], preferred_element_type=f32)[0]


def tail(x_t, g):
    depth, rows = x_t.shape
    cols = g.shape[1]
    step = depth // 3
    return pl.pallas_call(
        tail_kernel,
        grid=(3,),
        in_specs=[
            pl.BlockSpec((step, rows), lambda i: (i, 0)),
            pl.BlockSpec((rows, cols), lambda i: (0, 0)),
        ],
        out_specs=[
            pl.BlockSpec((step, cols), lambda i: (i, 0)),
            pl.BlockSpec((cols,), lambda i: (0,)),
        ],
        out_shape=[
            jax.ShapeDtypeStruct((depth, cols), bf16),
            jax.ShapeDtypeStruct((cols,), f32),
        ],
        compiler_params=pltpu.CompilerParams(vmem_limit_bytes=24 * 2**20),
    )(x_t, g)


def body(tokens, enc_weight, enc_bias, dec_weight, pairs, counts):
    rows, width = tokens.shape
    local_lat = enc_weight.shape[1]
    nblk = local_lat // BL
    slots = pairs.shape[1]
    n_lat = lax.axis_size("lat")
    n_tok = lax.axis_size("tok")
    lat = lax.axis_index("lat")
    tok = lax.axis_index("tok")
    half = tok * 2 // n_tok
    own = rows // n_tok
    share = rows // n_lat
    side = round(n_lat**0.5)
    n_x = n_tok // 2
    even = tok % 2 == 0
    y, z = lat // side, lat % side
    chunks = 2 * side
    chunk = rows // chunks
    both = ("lat", "tok")
    big, near, far = lat_groups(n_lat, n_tok)
    x_groups = [[2 * x + c for x in range(n_x)] for c in range(2)]
    c_groups = [[2 * x, 2 * x + 1] for x in range(n_x)]

    def gather_tok(v):
        spread = jnp.broadcast_to(v[None], (n_x,) + v.shape)
        got = exchange(spread, "tok", x_groups)
        return lax.all_gather(
            got.reshape(-1, local_lat), "tok", axis_index_groups=c_groups, axis=0, tiled=True
        )

    codes = pairs[0]
    valid = jnp.arange(slots, dtype=jnp.int32) < counts[0]
    g_own = tok * own // BR
    hit = valid[:, None] & (
        codes[:, None] == g_own * nblk + jnp.arange(local_lat, dtype=jnp.int32)[None, :] // BL
    )
    mask = jnp.any(hit, axis=0)[None, :]

    dec32 = dec_weight.astype(f32)
    squares = jnp.sum(dec32 * dec32, axis=1).astype(bf16)
    part = jnp.dot(tokens, enc_weight, preferred_element_type=f32).astype(bf16)
    part, squares = lax.optimization_barrier((part, squares))
    got = exchange(part.reshape(n_tok, own, local_lat), "tok", None)
    pre = jnp.sum(got.astype(f32), axis=0) + enc_bias[None, :]
    acts_own = jnp.where(mask, jax.nn.softplus(pre), 0.0).astype(bf16)
    extra = jnp.broadcast_to(squares[None, :], (EXTRA, local_lat))
    got = gather_tok(jnp.concatenate([acts_own, extra], axis=0))
    got = got.reshape(2, n_x, own + EXTRA, local_lat)
    acts = got[:, :, :own].reshape(rows, local_lat)
    sq = got[:, :, own].astype(f32)
    norm_a = jnp.sqrt(jnp.sum(sq[:, : n_x // 2], axis=(0, 1)) + EPSILON)
    norm_b = jnp.sqrt(jnp.sum(sq[:, n_x // 2 :], axis=(0, 1)) + EPSILON)
    own_norm = jnp.where(half == 0, norm_a, norm_b)

    recon = jnp.dot(acts, dec_weight, preferred_element_type=f32).astype(bf16)
    got = exchange(recon.reshape(chunks, chunk, width), both, big)
    line = jnp.sum(got.astype(f32), axis=0).astype(bf16)
    for groups in (near, far):
        two = lax.all_gather(line, both, axis_index_groups=groups, axis=0)
        total = jnp.sum(two.astype(f32), axis=0)
        line = total.astype(bf16)
    at = jnp.where(even, y % 2 * side + z, z % 2 * side + y) * chunk
    at = 2 * (at // own % n_x) * own + at // (n_x * own) * own + at % own
    x_line = lax.dynamic_slice_in_dim(tokens, at, chunk, 0)
    err_line = (total - x_line.astype(f32)).astype(bf16)
    err = exchange(jnp.broadcast_to(err_line[None], (chunks,) + err_line.shape), both, big)
    err = err.reshape(rows, width)

    back = lax.dot_general(
        err, dec_weight, (((1,), (1,)), ((), ())), preferred_element_type=f32
    ).astype(bf16)
    order = [[tok for group in x_groups for tok in group]]
    got = exchange(back.reshape(n_tok, own, local_lat), "tok", order)
    err_own = lax.dynamic_slice_in_dim(
        err, (y % 2 * n_x + y // 2) * own + z * share, share, 0
    )
    grad_act = jnp.sum(got.astype(f32), axis=0) + PENALTY * (norm_a + norm_b)[None, :]
    grad_own = jnp.where(mask, grad_act * jax.nn.sigmoid(pre), 0.0).astype(bf16)
    grad_pre = gather_tok(grad_own)

    act_sum = jnp.sum(acts.astype(f32), axis=0)
    dec_data = lax.dot_general(acts, err, (((0,), (0,)), ((), ())), preferred_element_type=f32)
    dec_grad = dec_data + PENALTY * (act_sum / own_norm)[:, None] * dec32
    tokens_t = tokens.reshape(n_x, 2, own, width).transpose(3, 1, 0, 2).reshape(width, rows)
    enc_grad, bias_grad = tail(tokens_t, grad_pre)
    return err_own, enc_grad, dec_grad.astype(bf16), bias_grad


def solution(mesh):
    return jax.shard_map(
        body,
        mesh=mesh,
        in_specs=(
            P(None, "tok"),
            P("tok", "lat"),
            P("lat"),
            P("lat", "tok"),
            P("lat", None),
            P("lat"),
        ),
        out_specs=(P("lat", "tok"), P("tok", "lat"), P("lat", "tok"), P("lat")),
        check_vma=False,
    )
```

```python
import jax
import jax.numpy as jnp
from jax import lax
from jax.experimental import pallas as pl
from jax.experimental.pallas import tpu as pltpu
from jax.sharding import PartitionSpec as P

BR = 128
BL = 64
PENALTY = 0.3
EPSILON = 1e-06
EXTRA = 8
PIECES = 4

f32 = jnp.float32
bf16 = jnp.bfloat16


def lat_groups(n_lat, n_tok):
    side = round(n_lat**0.5)
    quads = side // 2
    big, near, far = [], [], []
    for tok in range(n_tok):
        swap = tok % 2 == 1

        def device(a, p, b):
            pair = 2 * a + p
            lat = b * side + pair if swap else pair * side + b
            return lat * n_tok + tok

        for a in range(quads):
            big.append([device(a, p, b) for p in range(2) for b in range(side)])
        for p in range(2):
            for b in range(side):
                four = [device(a, p, b) for a in range(quads)]
                near += [four[:2], four[2:]]
                far += [four[1:3], [four[0], four[3]]]
    return big, near, far


def exchange(x, axis, groups):
    return lax.all_to_all(x, axis, 0, 0, axis_index_groups=groups, tiled=True)


def params():
    return pltpu.CompilerParams(vmem_limit_bytes=32 * 2**20)


HBM = pl.BlockSpec(memory_space=pltpu.HBM)
VMEM = pl.BlockSpec(memory_space=pltpu.VMEM)


def blocks(extent, count):
    size = extent // count
    return [pl.ds(i * size, size) for i in range(count)]


def tail_kernel(x_ref, g_ref, out_ref, bias_ref, out, sems):
    sent = []
    for i, m in enumerate(blocks(x_ref.shape[0], PIECES)):
        out[m] = jnp.dot(x_ref[m], g_ref[...], preferred_element_type=f32).astype(bf16)
        sent.append(pltpu.make_async_copy(out.at[m], out_ref.at[m], sems.at[i]))
        sent[i].start()
    ones = jnp.ones((8, g_ref.shape[0]), bf16)
    bias_ref[...] = jnp.dot(ones, g_ref[...], preferred_element_type=f32)[0]
    for copy in sent:
        copy.wait()


def tail(x_t, g):
    shape = (x_t.shape[0], g.shape[1])
    return pl.pallas_call(
        tail_kernel,
        in_specs=[VMEM, VMEM],
        out_specs=[HBM, pl.BlockSpec((g.shape[1],), lambda: (0,))],
        out_shape=[
            jax.ShapeDtypeStruct(shape, bf16),
            jax.ShapeDtypeStruct((g.shape[1],), f32),
        ],
        scratch_shapes=[pltpu.VMEM(shape, bf16), pltpu.SemaphoreType.DMA((PIECES,))],
        compiler_params=params(),
    )(x_t, g)


def body(tokens, enc_weight, enc_bias, dec_weight, pairs, counts):
    rows, width = tokens.shape
    local_lat = enc_weight.shape[1]
    nblk = local_lat // BL
    slots = pairs.shape[1]
    n_lat = lax.axis_size("lat")
    n_tok = lax.axis_size("tok")
    lat = lax.axis_index("lat")
    tok = lax.axis_index("tok")
    half = tok * 2 // n_tok
    own = rows // n_tok
    share = rows // n_lat
    side = round(n_lat**0.5)
    n_x = n_tok // 2
    even = tok % 2 == 0
    y, z = lat // side, lat % side
    chunks = 2 * side
    chunk = rows // chunks
    both = ("lat", "tok")
    big, near, far = lat_groups(n_lat, n_tok)
    x_groups = [[2 * x + c for x in range(n_x)] for c in range(2)]
    c_groups = [[2 * x, 2 * x + 1] for x in range(n_x)]

    def gather_tok(v):
        spread = jnp.broadcast_to(v[None], (n_x,) + v.shape)
        got = exchange(spread, "tok", x_groups)
        return lax.all_gather(
            got.reshape(-1, local_lat), "tok", axis_index_groups=c_groups, axis=0, tiled=True
        )

    codes = pairs[0]
    valid = jnp.arange(slots, dtype=jnp.int32) < counts[0]
    g_own = tok * own // BR
    hit = valid[:, None] & (
        codes[:, None] == g_own * nblk + jnp.arange(local_lat, dtype=jnp.int32)[None, :] // BL
    )
    mask = jnp.any(hit, axis=0)[None, :]

    part = jnp.dot(tokens, enc_weight, preferred_element_type=f32).astype(bf16)
    part, dec_late = lax.optimization_barrier((part, dec_weight))
    dec32 = dec_late.astype(f32)
    squares = jnp.sum(dec32 * dec32, axis=1).astype(bf16)
    got = exchange(part.reshape(n_tok, own, local_lat), "tok", None)
    pre = jnp.sum(got.astype(f32), axis=0) + enc_bias[None, :]
    acts_own = jnp.where(mask, jax.nn.softplus(pre), 0.0).astype(bf16)
    extra = jnp.broadcast_to(squares[None, :], (EXTRA, local_lat))
    got = gather_tok(jnp.concatenate([acts_own, extra], axis=0))
    got = got.reshape(2, n_x, own + EXTRA, local_lat)
    acts = got[:, :, :own].reshape(rows, local_lat)
    sq = got[:, :, own].astype(f32)
    norm_a = jnp.sqrt(jnp.sum(sq[:, : n_x // 2], axis=(0, 1)) + EPSILON)
    norm_b = jnp.sqrt(jnp.sum(sq[:, n_x // 2 :], axis=(0, 1)) + EPSILON)
    own_norm = jnp.where(half == 0, norm_a, norm_b)

    recon = jnp.dot(acts, dec_late, preferred_element_type=f32).astype(bf16)
    got = exchange(recon.reshape(chunks, chunk, width), both, big)
    line = jnp.sum(got.astype(f32), axis=0).astype(bf16)
    for groups in (near, far):
        two = lax.all_gather(line, both, axis_index_groups=groups, axis=0)
        total = jnp.sum(two.astype(f32), axis=0)
        line = total.astype(bf16)
    at = jnp.where(even, y % 2 * side + z, z % 2 * side + y) * chunk
    at = 2 * (at // own % n_x) * own + at // (n_x * own) * own + at % own
    x_line = lax.dynamic_slice_in_dim(tokens, at, chunk, 0)
    err_line = (total - x_line.astype(f32)).astype(bf16)
    err = exchange(jnp.broadcast_to(err_line[None], (chunks,) + err_line.shape), both, big)
    err = err.reshape(rows, width)

    back = lax.dot_general(
        err, dec_weight, (((1,), (1,)), ((), ())), preferred_element_type=f32
    ).astype(bf16)
    order = [[tok for group in x_groups for tok in group]]
    got = exchange(back.reshape(n_tok, own, local_lat), "tok", order)
    err_own = lax.dynamic_slice_in_dim(
        err, (y % 2 * n_x + y // 2) * own + z * share, share, 0
    )
    grad_act = jnp.sum(got.astype(f32), axis=0) + PENALTY * (norm_a + norm_b)[None, :]
    grad_own = jnp.where(mask, grad_act * jax.nn.sigmoid(pre), 0.0).astype(bf16)
    grad_pre = gather_tok(grad_own)

    act_sum = jnp.sum(acts.astype(f32), axis=0)
    dec_data = lax.dot_general(acts, err, (((0,), (0,)), ((), ())), preferred_element_type=f32)
    dec_grad = dec_data + PENALTY * (act_sum / own_norm)[:, None] * dec32
    tokens_t = tokens.reshape(n_x, 2, own, width).transpose(3, 1, 0, 2).reshape(width, rows)
    enc_grad, bias_grad = tail(tokens_t, grad_pre)
    return err_own, enc_grad, dec_grad.astype(bf16), bias_grad


def solution(mesh):
    return jax.shard_map(
        body,
        mesh=mesh,
        in_specs=(
            P(None, "tok"),
            P("tok", "lat"),
            P("lat"),
            P("lat", "tok"),
            P("lat", None),
            P("lat"),
        ),
        out_specs=(P("lat", "tok"), P("tok", "lat"), P("lat", "tok"), P("lat")),
        check_vma=False,
    )
```

```python
import jax
import jax.numpy as jnp
from jax import lax
from jax.experimental import pallas as pl
from jax.experimental.pallas import tpu as pltpu
from jax.sharding import PartitionSpec as P

BR = 128
BL = 64
PENALTY = 0.3
EPSILON = 1e-06
EXTRA = 8
PIECES = 4

f32 = jnp.float32
bf16 = jnp.bfloat16


def lat_groups(n_lat, n_tok):
    side = round(n_lat**0.5)
    quads = side // 2
    big, small = [], []
    for tok in range(n_tok):
        swap = tok % 2 == 1

        def device(a, p, b):
            pair = 2 * a + p
            lat = b * side + pair if swap else pair * side + b
            return lat * n_tok + tok

        for a in range(quads):
            big.append([device(a, p, b) for p in range(2) for b in range(side)])
        for p in range(2):
            for b in range(side):
                four = [device(a, p, b) for a in range(quads)]
                small.append(four)
    return big, small


def exchange(x, axis, groups):
    return lax.all_to_all(x, axis, 0, 0, axis_index_groups=groups, tiled=True)


def params():
    return pltpu.CompilerParams(vmem_limit_bytes=32 * 2**20)


HBM = pl.BlockSpec(memory_space=pltpu.HBM)
VMEM = pl.BlockSpec(memory_space=pltpu.VMEM)


def blocks(extent, count):
    size = extent // count
    return [pl.ds(i * size, size) for i in range(count)]


def tail_kernel(x_ref, g_ref, out_ref, bias_ref, out, sems):
    sent = []
    for i, m in enumerate(blocks(x_ref.shape[0], PIECES)):
        out[m] = jnp.dot(x_ref[m], g_ref[...], preferred_element_type=f32).astype(bf16)
        sent.append(pltpu.make_async_copy(out.at[m], out_ref.at[m], sems.at[i]))
        sent[i].start()
    ones = jnp.ones((8, g_ref.shape[0]), bf16)
    bias_ref[...] = jnp.dot(ones, g_ref[...], preferred_element_type=f32)[0]
    for copy in sent:
        copy.wait()


def tail(x_t, g):
    shape = (x_t.shape[0], g.shape[1])
    return pl.pallas_call(
        tail_kernel,
        in_specs=[VMEM, VMEM],
        out_specs=[HBM, pl.BlockSpec((g.shape[1],), lambda: (0,))],
        out_shape=[
            jax.ShapeDtypeStruct(shape, bf16),
            jax.ShapeDtypeStruct((g.shape[1],), f32),
        ],
        scratch_shapes=[pltpu.VMEM(shape, bf16), pltpu.SemaphoreType.DMA((PIECES,))],
        compiler_params=params(),
    )(x_t, g)


def body(tokens, enc_weight, enc_bias, dec_weight, pairs, counts):
    rows, width = tokens.shape
    local_lat = enc_weight.shape[1]
    nblk = local_lat // BL
    slots = pairs.shape[1]
    n_lat = lax.axis_size("lat")
    n_tok = lax.axis_size("tok")
    lat = lax.axis_index("lat")
    tok = lax.axis_index("tok")
    half = tok * 2 // n_tok
    own = rows // n_tok
    share = rows // n_lat
    side = round(n_lat**0.5)
    n_x = n_tok // 2
    even = tok % 2 == 0
    y, z = lat // side, lat % side
    chunks = 2 * side
    chunk = rows // chunks
    both = ("lat", "tok")
    big, small = lat_groups(n_lat, n_tok)
    x_groups = [[2 * x + c for x in range(n_x)] for c in range(2)]
    c_groups = [[2 * x, 2 * x + 1] for x in range(n_x)]

    def gather_tok(v):
        spread = jnp.broadcast_to(v[None], (n_x,) + v.shape)
        got = exchange(spread, "tok", x_groups)
        return lax.all_gather(
            got.reshape(-1, local_lat), "tok", axis_index_groups=c_groups, axis=0, tiled=True
        )

    codes = pairs[0]
    valid = jnp.arange(slots, dtype=jnp.int32) < counts[0]
    g_own = tok * own // BR
    hit = valid[:, None] & (
        codes[:, None] == g_own * nblk + jnp.arange(local_lat, dtype=jnp.int32)[None, :] // BL
    )
    mask = jnp.any(hit, axis=0)[None, :]

    part = jnp.dot(tokens, enc_weight, preferred_element_type=f32).astype(bf16)
    part, dec_late = lax.optimization_barrier((part, dec_weight))
    dec32 = dec_late.astype(f32)
    squares = jnp.sum(dec32 * dec32, axis=1).astype(bf16)
    got = exchange(part.reshape(n_tok, own, local_lat), "tok", None)
    pre = jnp.sum(got.astype(f32), axis=0) + enc_bias[None, :]
    acts_own = jnp.where(mask, jax.nn.softplus(pre), 0.0).astype(bf16)
    extra = jnp.broadcast_to(squares[None, :], (EXTRA, local_lat))
    got = gather_tok(jnp.concatenate([acts_own, extra], axis=0))
    got = got.reshape(2, n_x, own + EXTRA, local_lat)
    acts = got[:, :, :own].reshape(rows, local_lat)
    sq = got[:, :, own].astype(f32)
    norm_a = jnp.sqrt(jnp.sum(sq[:, : n_x // 2], axis=(0, 1)) + EPSILON)
    norm_b = jnp.sqrt(jnp.sum(sq[:, n_x // 2 :], axis=(0, 1)) + EPSILON)
    own_norm = jnp.where(half == 0, norm_a, norm_b)

    recon = jnp.dot(acts, dec_late, preferred_element_type=f32).astype(bf16)
    got = exchange(recon.reshape(chunks, chunk, width), both, big)
    line = jnp.sum(got.astype(f32), axis=0).astype(bf16)
    got = exchange(jnp.broadcast_to(line[None], (side // 2,) + line.shape), both, small)
    total = jnp.sum(got.astype(f32), axis=0)
    at = jnp.where(even, y % 2 * side + z, z % 2 * side + y) * chunk
    at = 2 * (at // own % n_x) * own + at // (n_x * own) * own + at % own
    x_line = lax.dynamic_slice_in_dim(tokens, at, chunk, 0)
    err_line = (total - x_line.astype(f32)).astype(bf16)
    err = exchange(jnp.broadcast_to(err_line[None], (chunks,) + err_line.shape), both, big)
    err = err.reshape(rows, width)

    back = lax.dot_general(
        err, dec_weight, (((1,), (1,)), ((), ())), preferred_element_type=f32
    ).astype(bf16)
    order = [[tok for group in x_groups for tok in group]]
    got = exchange(back.reshape(n_tok, own, local_lat), "tok", order)
    err_own = lax.dynamic_slice_in_dim(
        err, (y % 2 * n_x + y // 2) * own + z * share, share, 0
    )
    grad_act = jnp.sum(got.astype(f32), axis=0) + PENALTY * (norm_a + norm_b)[None, :]
    grad_own = jnp.where(mask, grad_act * jax.nn.sigmoid(pre), 0.0).astype(bf16)
    grad_pre = gather_tok(grad_own)

    act_sum = jnp.sum(acts.astype(f32), axis=0)
    dec_data = lax.dot_general(acts, err, (((0,), (0,)), ((), ())), preferred_element_type=f32)
    dec_grad = dec_data + PENALTY * (act_sum / own_norm)[:, None] * dec32
    tokens_t = tokens.reshape(n_x, 2, own, width).transpose(3, 1, 0, 2).reshape(width, rows)
    enc_grad, bias_grad = tail(tokens_t, grad_pre)
    return err_own, enc_grad, dec_grad.astype(bf16), bias_grad


def solution(mesh):
    return jax.shard_map(
        body,
        mesh=mesh,
        in_specs=(
            P(None, "tok"),
            P("tok", "lat"),
            P("lat"),
            P("lat", "tok"),
            P("lat", None),
            P("lat"),
        ),
        out_specs=(P("lat", "tok"), P("tok", "lat"), P("lat", "tok"), P("lat")),
        check_vma=False,
    )
```
